512 devices in a mesh: blk: 32 (over x, z_lo, core), narrow: 16 (over z_hi, y).
Axes of the slice: x: 4, y: 8, z: 8 (z_hi: 2, z_lo: 4; z = z_hi * 4 + z_lo), core: 2. Of those that a mesh axis runs over, the one named last changes fastest.
Arguments:
- user_factors: float32 [131072, 128], P(('blk', 'narrow')), may hold values from -2 to 2
- user_m: float32 [131072, 128], P(('blk', 'narrow')), may hold values from -1.75 to 1.75
- user_v: float32 [131072, 128], P(('blk', 'narrow')), may hold values from 0.05 to 1
- item_factors: float32 [131072, 128], P(('blk', 'narrow')), may hold values from -2 to 2
- item_m: float32 [131072, 128], P(('blk', 'narrow')), may hold values from -1.75 to 1.75
- item_v: float32 [131072, 128], P(('blk', 'narrow')), may hold values from 0.05 to 1
- ratings: bfloat16 [32, 16, 3, 36, 128, 128], P('blk', 'narrow'), may hold values from -6 to 6
- user_tiles: int32 [32, 16, 3, 36], P('blk', 'narrow'), may hold values from 0 to 1, as said below
- item_tiles: int32 [32, 16, 3, 36], P('blk', 'narrow'), may hold values from 0 to 31
- tile_counts: int32 [32, 16, 3], P('blk', 'narrow'), may hold values from 4 to 36, as said below
Outputs:
- new_user_factors: float32 [131072, 128], P(('blk', 'narrow'))
- new_user_m: float32 [131072, 128], P(('blk', 'narrow'))
- new_user_v: float32 [131072, 128], P(('blk', 'narrow'))
- new_item_factors: float32 [131072, 128], P(('blk', 'narrow'))
- new_item_m: float32 [131072, 128], P(('blk', 'narrow'))
- new_item_v: float32 [131072, 128], P(('blk', 'narrow'))
The draws below stay inside these ranges and needn't reach their ends.
Inputs may be any that keep to these rules, and one draw needn't show every extreme that they name: Slots may name the same pair (user_tiles, item_tiles) more than once. Only the first tile_counts slots are live; in every sub-step some device has all 36 slots live.
All inputs are finite; a program needn't handle non-finite values.
Results may differ from the reference program's by a relative error of at most 0.02.
Values may be sent and summed in bfloat16 or wider, within the bound.
No kernel may reach another device: no remote copies, remote signals or barrier semaphores. Data moves between devices by JAX's collectives and lax.ppermute only.
A program may use at most 64 MiB of HBM per device.

```python
import math
import jax
import jax.numpy as jnp
from jax import lax

K = 128
TILE = 128
I_OWN = 256
U_DEV = 256
MAXT = 36
STEPS = 3
I_BLK = 4096
ITEMS = 131072
USERS = 131072
N_BLK = 32
N_NARROW = 16


def pair_codes(key):
    user_count = U_DEV // TILE
    item_count = I_OWN * N_NARROW // TILE
    codes = jax.random.randint(key, (N_BLK, N_NARROW, STEPS, MAXT), 0, user_count * item_count)
    return (codes.astype(jnp.int32), item_count)


def draw_user_tiles(key, part):
    codes, item_count = pair_codes(key)
    return (codes // item_count).astype(jnp.int32)


def draw_item_tiles(key, part):
    codes, item_count = pair_codes(key)
    return (codes % item_count).astype(jnp.int32)


def draw_tile_counts(key, part):
    key = jax.random.fold_in(key, 7)
    first_key, second_key = jax.random.split(key)
    powers = jax.random.randint(first_key, (N_BLK * N_NARROW, STEPS), 0, 4)
    counts = jnp.maximum(MAXT // jnp.left_shift(1, powers), 1)
    chosen = jax.random.randint(second_key, (STEPS,), 0, N_BLK * N_NARROW)
    rows = jnp.arange(N_BLK * N_NARROW)[:, None]
    counts = jnp.where(rows == chosen[None, :], MAXT, counts)
    return counts.reshape(N_BLK, N_NARROW, STEPS).astype(jnp.int32)


def block_levels(own_key, dims, cuts, least, largest):
    loudness = 1.0
    for axis_at, blocks in cuts:
        heights = jax.random.uniform(jax.random.fold_in(jax.random.fold_in(own_key, 6), axis_at), (blocks,), jnp.float32, least / len(cuts), largest / len(cuts))
        loudness = loudness * jnp.repeat(jnp.exp(heights), dims[axis_at] // blocks).reshape((-1,) + (1,) * (len(dims) - 1 - axis_at))
    return loudness


def normal_values(rng, dims, spread, reach, cuts=(), kind=jnp.bfloat16):
    drawn = jax.random.normal(rng, dims, jnp.float32) * spread
    if len(cuts) > 0:
        drawn = block_levels(rng, dims, cuts, -0.22, 0.18) * drawn
    return jnp.clip(drawn, min=-reach, max=reach).astype(kind)


def setup_inputs(seed: int = 0) -> dict:
    seeds = jax.random.split(jax.random.key(seed), 11)
    user_factors = normal_values(seeds[0], (USERS, K), 0.35, 2.0, ((0, 512),), jnp.float32)
    user_m = normal_values(seeds[1], (USERS, K), 0.3, 1.75, ((0, 512),), jnp.float32)
    user_v = jnp.clip(jnp.exp(math.log(1.0) - 2.9957323 * jax.random.uniform(seeds[2], (USERS, K), jnp.float32) ** block_levels(seeds[2], (USERS, K), ((0, 512),), -0.2, 0.2)), 0.05, 1.0)
    item_factors = normal_values(seeds[3], (ITEMS, K), 0.35, 2.0, ((0, 512),), jnp.float32)
    item_m = normal_values(seeds[4], (ITEMS, K), 0.3, 1.75, ((0, 512),), jnp.float32)
    item_v = jnp.clip(jnp.exp(math.log(1.0) - 2.9957323 * jax.random.uniform(seeds[5], (ITEMS, K), jnp.float32) ** block_levels(seeds[5], (ITEMS, K), ((0, 512),), -0.2, 0.2)), 0.05, 1.0)
    ratings = normal_values(seeds[6], (N_BLK, N_NARROW, STEPS, MAXT, TILE, TILE), 1.0, 6.0, ((0, 32), (1, 16)))
    user_tiles = draw_user_tiles(jax.random.fold_in(seeds[10], 71), 0)
    item_tiles = draw_item_tiles(jax.random.fold_in(seeds[10], 71), 0)
    tile_counts = draw_tile_counts(jax.random.fold_in(seeds[10], 71), 0)
    return dict(user_factors=user_factors, user_m=user_m, user_v=user_v, item_factors=item_factors, item_m=item_m, item_v=item_v, ratings=ratings, user_tiles=user_tiles, item_tiles=item_tiles, tile_counts=tile_counts)


LEARN_RATE = 0.01
BETA_ONE = 0.8
BETA_TWO = 0.95
ADAM_EPS = 1e-08
DECAY_REG = 0.05
GRAD_SCALE = 0.03125

def adam_update(param, first, second, grad):
    first = BETA_ONE * first + (1.0 - BETA_ONE) * grad
    second = BETA_TWO * second + (1.0 - BETA_TWO) * grad * grad
    return (param - LEARN_RATE * first / (jnp.sqrt(second) + ADAM_EPS), first, second)

def tile_terms(user_bf, item_bf, rating_tiles, user_idx, item_idx, count):
    user_rows = user_bf.reshape(U_DEV // TILE, TILE, K)[user_idx].astype(jnp.float32)
    item_rows = item_bf.reshape(I_BLK // TILE, TILE, K)[item_idx].astype(jnp.float32)
    predicted = jnp.einsum('tak,tbk->tab', user_rows, item_rows)
    live = (jnp.arange(MAXT) < count).astype(jnp.float32)
    errors = ((predicted - rating_tiles.astype(jnp.float32)) * live[:, None, None]).astype(jnp.bfloat16)
    errors = lax.optimization_barrier(errors).astype(jnp.float32)
    user_part = jnp.einsum('tab,tbk->tak', errors, item_rows)
    item_part = jnp.einsum('tab,tak->tbk', errors, user_rows)
    user_grad = jnp.zeros((U_DEV // TILE, TILE, K), jnp.float32).at[user_idx].add(user_part)
    item_grad = jnp.zeros((I_BLK // TILE, TILE, K), jnp.float32).at[item_idx].add(item_part)
    return (user_grad.reshape(U_DEV, K), item_grad.reshape(I_BLK, K))

def stratum(values):
    user_fac, user_first, user_second, item_fac, item_first, item_second, rat, user_idx, item_idx, counts = values
    user_bf = user_fac.astype(jnp.bfloat16)
    item_bf = item_fac.astype(jnp.bfloat16)
    user_grad, item_part = jax.vmap(tile_terms, in_axes=(0, None, 0, 0, 0, 0))(user_bf, item_bf, rat, user_idx, item_idx, counts)
    user_fac, user_first, user_second = adam_update(user_fac, user_first, user_second, GRAD_SCALE * user_grad + DECAY_REG * user_fac)
    rounded = lax.optimization_barrier(item_part.astype(jnp.bfloat16)).astype(jnp.float32)
    item_total = lax.optimization_barrier(jnp.sum(rounded, axis=0))
    item_fac, item_first, item_second = adam_update(item_fac, item_first, item_second, GRAD_SCALE * item_total + DECAY_REG * item_fac)
    return (user_fac, user_first, user_second, item_fac, item_first, item_second)

def reference(user_factors, user_m, user_v, item_factors, item_m, item_v, ratings, user_tiles, item_tiles, tile_counts):
    user_state = [arr.reshape(N_BLK, N_NARROW, U_DEV, K) for arr in (user_factors, user_m, user_v)]
    item_state = [arr.reshape(N_BLK, I_BLK, K) for arr in (item_factors, item_m, item_v)]
    for substep in range(STEPS):
        current = [jnp.roll(arr, -substep, axis=0) for arr in item_state]
        result = lax.map(stratum, (user_state[0], user_state[1], user_state[2], current[0], current[1], current[2], ratings[:, :, substep], user_tiles[:, :, substep], item_tiles[:, :, substep], tile_counts[:, :, substep]))
        user_state = [result[0], result[1], result[2]]
        item_state = [jnp.roll(arr, substep, axis=0) for arr in (result[3], result[4], result[5])]
    users_out = [arr.reshape(USERS, K) for arr in user_state]
    items_out = [jnp.roll(arr, -(STEPS - 1), axis=0).reshape(ITEMS, K) for arr in item_state]
    return (users_out[0], users_out[1], users_out[2], items_out[0], items_out[1], items_out[2])
```

```python
import jax
import jax.numpy as jnp
from jax import lax
from jax.sharding import PartitionSpec as P

K = 128
TILE = 128
MAXT = 36
STEPS = 3


LEARN_RATE = 0.01
BETA_ONE = 0.8
BETA_TWO = 0.95
ADAM_EPS = 1e-08
DECAY_REG = 0.05
GRAD_SCALE = 0.03125


def shifted(block, axis, distance):
    devices = range(lax.axis_size(axis))
    route = [((i - distance) % len(devices), i) for i in devices]
    return lax.ppermute(block, axis, route)


def gathered(rows):
    members = lax.axis_size("narrow")
    copies = jnp.broadcast_to(rows[None], (members,) + rows.shape)
    return lax.all_to_all(copies, "narrow", 0, 0).reshape(members * rows.shape[0], K)


def summed(partial):
    members = lax.axis_size("narrow")
    parts = partial.reshape(members, partial.shape[0] // members, K)
    arrived = lax.all_to_all(parts, "narrow", 0, 0)
    return jnp.sum(arrived.astype(jnp.float32), axis=0)


def adam_update(param, first, second, grad):
    first = BETA_ONE * first + (1.0 - BETA_ONE) * grad
    second = BETA_TWO * second + (1.0 - BETA_TWO) * grad * grad
    return (param - LEARN_RATE * first / (jnp.sqrt(second) + ADAM_EPS), first, second)


def slot_terms(user_bf, item_bf, rating_tiles, user_idx, item_idx, count):
    user_tiles_all = user_bf.shape[0] // TILE
    item_tiles_all = item_bf.shape[0] // TILE
    user_rows = user_bf.reshape(user_tiles_all, TILE, K)[user_idx]
    item_rows = item_bf.reshape(item_tiles_all, TILE, K)[item_idx]
    predicted = jnp.einsum("tak,tbk->tab", user_rows, item_rows, preferred_element_type=jnp.float32)
    live = (jnp.arange(MAXT) < count).astype(jnp.float32)
    errors = ((predicted - rating_tiles.astype(jnp.float32)) * live[:, None, None]).astype(
        jnp.bfloat16
    )
    user_part = jnp.einsum("tab,tbk->tak", errors, item_rows, preferred_element_type=jnp.float32)
    item_part = jnp.einsum("tab,tak->tbk", errors, user_rows, preferred_element_type=jnp.float32)
    user_select = (jnp.arange(user_tiles_all)[:, None] == user_idx[None, :]).astype(jnp.float32)
    user_grad = jnp.dot(
        user_select, user_part.reshape(MAXT, TILE * K), precision=lax.Precision.HIGHEST
    )
    return (user_grad.reshape(user_bf.shape[0], K), item_part.reshape(MAXT, TILE * K))


def select_rows(item_part, item_idx, start, count):
    tiles = count // TILE
    wanted = start // TILE + jnp.arange(tiles, dtype=jnp.int32)
    selector = (wanted[:, None] == item_idx[None, :]).astype(jnp.float32)
    return jnp.dot(selector, item_part, precision=lax.Precision.HIGHEST).reshape(count, K)


def per_device(
    user_factors,
    user_m,
    user_v,
    item_factors,
    item_m,
    item_v,
    ratings,
    user_tiles,
    item_tiles,
    tile_counts,
):
    user_fac, user_first, user_second = (user_factors, user_m, user_v)
    item_fac, item_first, item_second = (item_factors, item_m, item_v)
    for substep in range(STEPS):
        current_rows = gathered(item_fac.astype(jnp.bfloat16))
        block_rows = current_rows.shape[0]
        item_idx = item_tiles[0, 0, substep]
        user_grad, item_part = slot_terms(
            user_fac.astype(jnp.bfloat16),
            current_rows,
            ratings[0, 0, substep],
            user_tiles[0, 0, substep],
            item_idx,
            tile_counts[0, 0, substep],
        )
        user_fac, user_first, user_second = adam_update(
            user_fac, user_first, user_second, GRAD_SCALE * user_grad + DECAY_REG * user_fac
        )
        dense_part = select_rows(item_part, item_idx, 0, block_rows)
        item_total = summed(dense_part.astype(jnp.bfloat16))
        item_fac, item_first, item_second = adam_update(
            item_fac, item_first, item_second, GRAD_SCALE * item_total + DECAY_REG * item_fac
        )
        if substep + 1 < STEPS:
            item_fac, item_first, item_second = shifted(
                (item_fac, item_first, item_second), "blk", -1
            )
    return (user_fac, user_first, user_second, item_fac, item_first, item_second)


def solution(mesh):
    return jax.shard_map(
        per_device,
        mesh=mesh,
        in_specs=(
            P(("blk", "narrow"), None),
            P(("blk", "narrow"), None),
            P(("blk", "narrow"), None),
            P(("blk", "narrow"), None),
            P(("blk", "narrow"), None),
            P(("blk", "narrow"), None),
            P("blk", "narrow", None, None, None, None),
            P("blk", "narrow", None, None),
            P("blk", "narrow", None, None),
            P("blk", "narrow", None),
        ),
        out_specs=(
            P(("blk", "narrow"), None),
            P(("blk", "narrow"), None),
            P(("blk", "narrow"), None),
            P(("blk", "narrow"), None),
            P(("blk", "narrow"), None),
            P(("blk", "narrow"), None),
        ),
        check_vma=False,
    )
```

```python
import jax
import jax.numpy as jnp
from jax import lax
from jax.experimental import pallas as pl
from jax.experimental.pallas import tpu as pltpu
from jax.sharding import PartitionSpec as P

K = 128
TILE = 128
MAXT = 36
STEPS = 3
RING = 8
USER_ROWS = 256
ITEM_ROWS = 256
USER_TILES = 2
ITEM_TILES = 32
COUNT_ROWS = 16
PART = USER_ROWS + COUNT_ROWS


LEARN_RATE = 0.01
BETA_ONE = 0.8
BETA_TWO = 0.95
ADAM_EPS = 1e-08
DECAY_REG = 0.05
GRAD_SCALE = 0.03125

VMEM = pl.BlockSpec(memory_space=pltpu.VMEM)
SMEM = pl.BlockSpec(memory_space=pltpu.SMEM)
F32 = jnp.float32
BF16 = jnp.bfloat16


def adam_update(param, first, second, grad):
    first = BETA_ONE * first + (1.0 - BETA_ONE) * grad
    second = BETA_TWO * second + (1.0 - BETA_TWO) * grad * grad
    return (param - LEARN_RATE * first / (jnp.sqrt(second) + ADAM_EPS), first, second)


def kernel_call(body, outs, in_specs, scratch=(), flops=0, moved=1 << 20):
    return pl.pallas_call(
        body,
        out_shape=outs,
        in_specs=in_specs,
        out_specs=jax.tree.map(lambda _: VMEM, outs),
        scratch_shapes=list(scratch),
        cost_estimate=pl.CostEstimate(flops=flops, bytes_accessed=moved, transcendentals=0),
        compiler_params=pltpu.CompilerParams(vmem_limit_bytes=40 << 20),
    )


def dense_body(slots_ref, live_ref, ratings_ref, out_ref, total):
    total[...] = jnp.zeros_like(total)

    def add(t, carry):
        row = pl.multiple_of(slots_ref[t] * TILE, TILE)
        total[pl.ds(row, TILE), :] += ratings_ref[t].astype(F32)
        return carry

    lax.fori_loop(0, live_ref[0], add, 0)
    out_ref[...] = total[...].astype(BF16)


def dense_ratings(slots, live, ratings):
    rows = ITEM_TILES * USER_ROWS
    return kernel_call(
        dense_body,
        jax.ShapeDtypeStruct((rows, TILE), BF16),
        [SMEM, SMEM, VMEM],
        [pltpu.VMEM((rows, TILE), F32)],
        moved=10 << 20,
    )(slots, live, ratings)


def rating_part_body(order_ref, users_ref, dense_ref, out_ref):
    users = users_ref[: USER_ROWS]
    for k in range(ITEM_TILES):
        row = pl.multiple_of(order_ref[k] * USER_ROWS, USER_ROWS)
        part = lax.dot_general(
            dense_ref[pl.ds(row, USER_ROWS), :],
            users,
            (((0,), (0,)), ((), ())),
            preferred_element_type=F32,
        )
        out_ref[k * TILE : (k + 1) * TILE] = part.astype(BF16)


def rating_part(order, users, dense):
    return kernel_call(
        rating_part_body,
        jax.ShapeDtypeStruct((ITEM_TILES * TILE, K), BF16),
        [SMEM, VMEM, VMEM],
        flops=2 * ITEM_TILES * USER_ROWS * TILE * K,
        moved=3 << 20,
    )(order, users, dense)


def user_body(order_ref, counts_ref, dense_ref, fac_ref, first_ref, second_ref, *rest):
    pieces, (fac_out, first_out, second_out, bf_out) = rest[:-4], rest[-4:]
    fac = fac_ref[...]
    users = fac.astype(BF16)
    total = jnp.zeros((USER_ROWS, K), F32)
    upper = lax.broadcasted_iota(jnp.int32, (USER_ROWS, TILE), 0) < TILE
    k = 0
    for piece in pieces:
        for pair in range(2):
            rows = piece[pair * ITEM_ROWS : (pair + 1) * ITEM_ROWS]
            predicted = lax.dot_general(
                users, rows, (((1,), (1,)), ((), ())), preferred_element_type=F32
            )
            errors = []
            for h in range(2):
                tile = order_ref[k]
                k += 1
                row = pl.multiple_of(tile * USER_ROWS, USER_ROWS)
                many = jnp.where(upper, counts_ref[tile], counts_ref[ITEM_TILES + tile])
                ratings = dense_ref[pl.ds(row, USER_ROWS), :].astype(F32)
                errors.append(
                    (predicted[:, h * TILE : (h + 1) * TILE] * many - ratings).astype(BF16)
                )
            total += jnp.dot(
                jnp.concatenate(errors, axis=1), rows, preferred_element_type=F32
            )
    grad = GRAD_SCALE * total + DECAY_REG * fac
    fac, first, second = adam_update(fac, first_ref[...], second_ref[...], grad)
    fac_out[...] = fac
    first_out[...] = first
    second_out[...] = second
    bf_out[...] = fac.astype(BF16)


def user_step(order, counts, dense, state, pieces):
    like = jax.ShapeDtypeStruct((USER_ROWS, K), F32)
    return kernel_call(
        user_body,
        (like, like, like, jax.ShapeDtypeStruct((USER_ROWS, K), BF16)),
        [SMEM, SMEM] + [VMEM] * (4 + len(pieces)),
        flops=4 * ITEM_TILES * USER_ROWS * TILE * K,
        moved=5 << 20,
    )(order, counts, dense, *state, *pieces)


def item_body(lanes_ref, own_ref, other_ref, fac_ref, first_ref, second_ref, *rest):
    pieces, (fac_out, first_out, second_out, bf_out) = rest[:-4], rest[-4:]
    lane = lax.broadcasted_iota(jnp.int32, (COUNT_ROWS, K), 1)
    weighted = [jnp.zeros((K, K), F32) for _ in range(2)]
    for piece, offset in pieces_at(pieces):
        for plane in range(2):
            top = offset + plane * PART
            counts = piece[top + USER_ROWS : top + PART].astype(F32)
            for u in range(USER_TILES):
                users = piece[top + u * TILE : top + (u + 1) * TILE]
                gram = lax.dot_general(
                    users, users, (((0,), (0,)), ((), ())), preferred_element_type=F32
                )
                for h in range(2):
                    at = u * ITEM_TILES + lanes_ref[0] + h
                    many = jnp.sum(jnp.where(lane == at, counts, 0.0), axis=1, keepdims=True)
                    weighted[h] = weighted[h] + many[0:1] * gram
    fac = fac_ref[...]
    rows = fac.astype(BF16)
    parts = []
    for h in range(2):
        high = weighted[h].astype(BF16)
        low = (weighted[h] - high.astype(F32)).astype(BF16)
        mine = rows[h * TILE : (h + 1) * TILE]
        parts.append(
            jnp.dot(mine, high, preferred_element_type=F32)
            + jnp.dot(mine, low, preferred_element_type=F32)
        )
    total = jnp.concatenate(parts, axis=0) - (
        own_ref[...].astype(F32) + other_ref[...].astype(F32)
    )
    grad = GRAD_SCALE * total + DECAY_REG * fac
    fac, first, second = adam_update(fac, first_ref[...], second_ref[...], grad)
    fac_out[...] = fac
    first_out[...] = first
    second_out[...] = second
    bf_out[...] = fac.astype(BF16)


def pieces_at(pieces):
    return [(p, 2 * ITEM_ROWS) for p in pieces[:-1]] + [(pieces[-1], 0)]


def item_step(lanes, own, other, state, pieces):
    like = jax.ShapeDtypeStruct((ITEM_ROWS, K), F32)
    return kernel_call(
        item_body,
        (like, like, like, jax.ShapeDtypeStruct((ITEM_ROWS, K), BF16)),
        [SMEM] + [VMEM] * (5 + len(pieces)),
        flops=2 * 32 * TILE * K * K,
        moved=4 << 20,
    )(lanes, own, other, *state, *pieces)


def per_device(
    user_factors,
    user_m,
    user_v,
    item_factors,
    item_m,
    item_v,
    ratings,
    user_tiles,
    item_tiles,
    tile_counts,
):
    strata = lax.axis_size("blk")
    narrow = lax.axis_index("narrow")
    plane, place = narrow // RING, narrow % RING
    forward = [(z * RING + y, z * RING + (y + 1) % RING) for z in range(2) for y in range(RING)]
    backward = [(target, source) for source, target in forward]
    across = [(n, (n + RING) % (2 * RING)) for n in range(2 * RING)]
    rings = [[z * RING + y for y in range(RING)] for z in range(2)]

    def to_earlier(value, swap):
        members = 2 * RING
        route = [
            (b * members + n, ((b - 1) % strata) * members + (n + swap) % members)
            for b in range(strata)
            for n in range(members)
        ]
        return lax.ppermute(value, ("blk", "narrow"), route)

    def tiles_of(places):
        owner = jnp.stack([plane, 1 - plane])[None, :, None] * RING + places[:, None, None]
        return (owner * 2 + jnp.arange(2)[None, None, :]).reshape(-1).astype(jnp.int32)

    distance = jnp.array([0, -1, 1, -2, 2, -3, 3, 4], jnp.int32)
    arrival = tiles_of((place + distance) % RING)
    by_place = tiles_of(jnp.arange(RING, dtype=jnp.int32))
    lanes = (narrow * 2).reshape(1).astype(jnp.int32)

    users_at, items_at, live = user_tiles[0, 0], item_tiles[0, 0], tile_counts[0, 0]
    alive = jnp.arange(MAXT)[None, :] < live[:, None]
    pair = users_at * ITEM_TILES + items_at
    slots = items_at * USER_TILES + users_at
    counts = jnp.sum(
        ((pair[:, :, None] == jnp.arange(K)[None, None, :]) & alive[:, :, None]).astype(F32), axis=1
    )
    count_rows = jnp.broadcast_to(counts[:, None, :], (STEPS, COUNT_ROWS, K)).astype(BF16)

    user_state = (user_factors, user_m, user_v)
    item_state = (item_factors, item_m, item_v)
    item_bf = item_factors.astype(BF16)
    user_bf = user_factors.astype(BF16)
    first = jnp.concatenate([user_bf, count_rows[0], item_bf], axis=0)
    arrived = lax.ppermute(first, "narrow", across)
    item_other, part_other = arrived[PART:], arrived[:PART]
    part_own = first[:PART]
    for s in range(STEPS):
        dense = dense_ratings(slots[s], live[s].reshape(1), ratings[0, 0, s])
        partial = lax.psum_scatter(
            rating_part(by_place, part_own, dense),
            "narrow",
            scatter_dimension=0,
            tiled=True,
            axis_index_groups=rings,
        )
        load = jnp.concatenate([item_bf, item_other, part_own, part_other], axis=0)
        pieces = [load]
        up = down = load
        for _ in range(3):
            up = lax.ppermute(up, "narrow", forward)
            down = lax.ppermute(down, "narrow", backward)
            pieces += [up, down]
        last_items = lax.ppermute(up[: 2 * ITEM_ROWS], "narrow", forward)
        last_users = lax.ppermute(down[2 * ITEM_ROWS :], "narrow", backward)
        other = lax.ppermute(partial[ITEM_ROWS:], "narrow", across)
        *item_state, item_bf = item_step(
            lanes, partial[:ITEM_ROWS], other, item_state, pieces + [last_users]
        )
        if s + 1 < STEPS:
            item_other = to_earlier(item_bf, RING)
            item_bf = to_earlier(item_bf, 0)
        *user_state, user_bf = user_step(
            arrival, counts[s], dense, user_state, pieces + [last_items]
        )
        if s + 1 < STEPS:
            part_own = jnp.concatenate([user_bf, count_rows[s + 1]], axis=0)
            part_other = lax.ppermute(part_own, "narrow", across)
            item_state = [to_earlier(array, 0) for array in item_state]
    return (*user_state, *item_state)


def solution(mesh):
    return jax.shard_map(
        per_device,
        mesh=mesh,
        in_specs=(
            P(("blk", "narrow"), None),
            P(("blk", "narrow"), None),
            P(("blk", "narrow"), None),
            P(("blk", "narrow"), None),
            P(("blk", "narrow"), None),
            P(("blk", "narrow"), None),
            P("blk", "narrow", None, None, None, None),
            P("blk", "narrow", None, None),
            P("blk", "narrow", None, None),
            P("blk", "narrow", None),
        ),
        out_specs=(
            P(("blk", "narrow"), None),
            P(("blk", "narrow"), None),
            P(("blk", "narrow"), None),
            P(("blk", "narrow"), None),
            P(("blk", "narrow"), None),
            P(("blk", "narrow"), None),
        ),
        check_vma=False,
    )
```

```python
import functools

import jax
import jax.numpy as jnp
from jax import lax
from jax.experimental import pallas as pl
from jax.experimental.pallas import tpu as pltpu
from jax.sharding import PartitionSpec as P

K = 128
TILE = 128
MAXT = 36
STEPS = 3
RING = 8
USER_ROWS = 256
ITEM_ROWS = 256
USER_TILES = 2
ITEM_TILES = 32
COUNT_ROWS = 16
PART = USER_ROWS + COUNT_ROWS
PAIRS = USER_TILES * ITEM_TILES
DISTANCES = (0, -1, 1, -2, 2, -3, 3, -4)


LEARN_RATE = 0.01
BETA_ONE = 0.8
BETA_TWO = 0.95
ADAM_EPS = 1e-08
DECAY_REG = 0.05
GRAD_SCALE = 0.03125

VMEM = pl.BlockSpec(memory_space=pltpu.VMEM)
SMEM = pl.BlockSpec(memory_space=pltpu.SMEM)
ANY = pl.BlockSpec(memory_space=pl.ANY)
F32 = jnp.float32
BF16 = jnp.bfloat16


def shape(rows, dtype=F32):
    return jax.ShapeDtypeStruct((rows, K), dtype)


def adam_update(param, first, second, grad):
    first = BETA_ONE * first + (1.0 - BETA_ONE) * grad
    second = BETA_TWO * second + (1.0 - BETA_TWO) * grad * grad
    return (param - LEARN_RATE * first / (jnp.sqrt(second) + ADAM_EPS), first, second)


def kernel_call(body, outs, in_specs, out_specs=None, scratch=(), flops=0, moved=1 << 20):
    return pl.pallas_call(
        body,
        out_shape=outs,
        in_specs=in_specs,
        out_specs=out_specs or jax.tree.map(lambda _: VMEM, outs),
        scratch_shapes=list(scratch),
        cost_estimate=pl.CostEstimate(flops=flops, bytes_accessed=moved, transcendentals=0),
        compiler_params=pltpu.CompilerParams(vmem_limit_bytes=40 << 20),
    )


def loaded(refs):
    if len(refs) == 3:
        return [ref[...] for ref in refs]
    return [refs[0][i * 256 : (i + 1) * 256] for i in range(3)]


def stored(refs, values):
    if len(refs) == 3:
        for ref, value in zip(refs, values):
            ref[...] = value
    else:
        for i, value in enumerate(values):
            refs[0][i * 256 : (i + 1) * 256] = value


def owned_tile(me, swap, place, half):
    plane = me // RING
    plane = 1 - plane if swap else plane
    return (plane * RING + place) * 2 + half


def opening_body(users_at, items_at, live, users, items, first_out, rows_out, counts_out):
    lane = lax.broadcasted_iota(jnp.int32, (COUNT_ROWS, K), 1)

    def clear(i, carry):
        counts_out[i] = 0.0
        return carry

    lax.fori_loop(0, STEPS * PAIRS, clear, 0)
    for s in range(STEPS):

        def add(t, row):
            pair = users_at[s * MAXT + t] * ITEM_TILES + items_at[s * MAXT + t]
            counts_out[s * PAIRS + pair] = counts_out[s * PAIRS + pair] + 1.0
            return row + jnp.where(lane == pair, 1.0, 0.0)

        row = lax.fori_loop(0, live[s], add, jnp.zeros((COUNT_ROWS, K), F32)).astype(BF16)
        if s == 0:
            first_out[USER_ROWS:PART] = row
        rows_out[s * COUNT_ROWS : (s + 1) * COUNT_ROWS] = row
    first_out[:USER_ROWS] = users[...].astype(BF16)
    first_out[PART:] = items[...].astype(BF16)


def opening(users_at, items_at, live, users, items):
    return kernel_call(
        opening_body,
        (
            shape(PART + ITEM_ROWS, BF16),
            shape(STEPS * COUNT_ROWS, BF16),
            jax.ShapeDtypeStruct((STEPS * PAIRS,), F32),
        ),
        [SMEM, SMEM, SMEM, VMEM, VMEM],
        (VMEM, VMEM, SMEM),
    )(users_at, items_at, live, users, items)


def joined_body(part, state, out):
    out[:PART] = part[...]
    out[PART:] = state[:ITEM_ROWS].astype(BF16)


def joined(part, state):
    return kernel_call(joined_body, shape(PART + ITEM_ROWS, BF16), [VMEM, VMEM])(part, state)


def packed_body(own, other, out):
    out[:ITEM_ROWS] = own[PART:]
    out[ITEM_ROWS : 2 * ITEM_ROWS] = other[PART:]
    out[2 * ITEM_ROWS : 2 * ITEM_ROWS + PART] = own[:PART]
    out[2 * ITEM_ROWS + PART :] = other[:PART]


def packed(own, other):
    return kernel_call(packed_body, shape(2 * (ITEM_ROWS + PART), BF16), [VMEM, VMEM])(own, other)


def dense_body(s, users_at, items_at, live, ratings, *rest):
    out_ref, total, tiles, sem = rest[-4:]
    fetch = pltpu.make_async_copy(ratings.at[0, 0, s], tiles, sem)
    fetch.start()
    total[...] = jnp.zeros_like(total)
    fetch.wait()

    def add(t, carry):
        slot = items_at[s * MAXT + t] * USER_TILES + users_at[s * MAXT + t]
        row = pl.multiple_of(slot * TILE, TILE)
        total[pl.ds(row, TILE), :] += tiles[t].astype(F32)
        return carry

    lax.fori_loop(0, live[s], add, 0)
    out_ref[...] = total[...].astype(BF16)


def dense_ratings(s, users_at, items_at, live, ratings, *later):
    rows = ITEM_TILES * USER_ROWS
    return kernel_call(
        functools.partial(dense_body, s),
        shape(rows, BF16),
        [SMEM, SMEM, SMEM, ANY] + [ANY] * len(later),
        scratch=[
            pltpu.VMEM((rows, TILE), F32),
            pltpu.VMEM((MAXT, TILE, TILE), BF16),
            pltpu.SemaphoreType.DMA,
        ],
        moved=10 << 20,
    )(users_at, items_at, live, ratings, *later)


def rating_part_body(me_ref, users_ref, dense_ref, out_ref):
    users = users_ref[:USER_ROWS]
    for k in range(ITEM_TILES):
        tile = owned_tile(me_ref[0], k // 2 % 2, k // 4, k % 2)
        row = pl.multiple_of(tile * USER_ROWS, USER_ROWS)
        part = lax.dot_general(
            dense_ref[pl.ds(row, USER_ROWS), :],
            users,
            (((0,), (0,)), ((), ())),
            preferred_element_type=F32,
        )
        out_ref[k * TILE : (k + 1) * TILE] = part.astype(BF16)


def rating_part(me, users, dense):
    return kernel_call(
        rating_part_body,
        shape(ITEM_TILES * TILE, BF16),
        [SMEM, VMEM, VMEM],
        flops=2 * ITEM_TILES * USER_ROWS * TILE * K,
        moved=3 << 20,
    )(me, users, dense)


def fetched(pieces, top, held, sems):
    rows = held.shape[1]
    copies = [
        pltpu.make_async_copy(piece.at[pl.ds(top, rows)], held.at[i], sems.at[i])
        for i, piece in enumerate(pieces)
    ]
    for copy in copies:
        copy.start()
    return copies


def fetch_scratch(rows):
    count = len(DISTANCES)
    return [pltpu.VMEM((count, rows, K), BF16), pltpu.SemaphoreType.DMA((count,))]


def user_body(s, states, me_ref, counts_ref, dense_ref, rows_ref, *rest):
    state_refs, pieces = rest[:states], rest[states : states + len(DISTANCES)]
    *outs, held, sems = rest[states + len(DISTANCES) :]
    outs = outs[-3:] if s + 1 == STEPS else outs[-2:]
    copies = fetched(pieces, 0, held, sems)
    fac, first, second = loaded(state_refs)
    users = fac.astype(BF16)
    total = jnp.zeros((USER_ROWS, K), F32)
    upper = lax.broadcasted_iota(jnp.int32, (USER_ROWS, TILE), 0) < TILE
    me = me_ref[0]
    for i, distance in enumerate(DISTANCES):
        copies[i].wait()
        place = (me % RING + distance + RING) % RING
        for swap in range(2):
            rows = held[i, swap * ITEM_ROWS : (swap + 1) * ITEM_ROWS]
            predicted = lax.dot_general(
                users, rows, (((1,), (1,)), ((), ())), preferred_element_type=F32
            )
            errors = []
            for h in range(2):
                tile = owned_tile(me, swap, place, h)
                row = pl.multiple_of(tile * USER_ROWS, USER_ROWS)
                at = s * PAIRS + tile
                many = jnp.where(upper, counts_ref[at], counts_ref[at + ITEM_TILES])
                ratings = dense_ref[pl.ds(row, USER_ROWS), :].astype(F32)
                errors.append(
                    (predicted[:, h * TILE : (h + 1) * TILE] * many - ratings).astype(BF16)
                )
            total += jnp.dot(
                jnp.concatenate(errors, axis=1), rows, preferred_element_type=F32
            )
    grad = GRAD_SCALE * total + DECAY_REG * fac
    fac, first, second = adam_update(fac, first, second, grad)
    if s + 1 < STEPS:
        part_out, *outs = outs
        part_out[:USER_ROWS] = fac.astype(BF16)
        part_out[USER_ROWS:] = rows_ref[(s + 1) * COUNT_ROWS : (s + 2) * COUNT_ROWS]
    stored(outs, (fac, first, second))


def user_step(s, me, counts, dense, rows, state, pieces, later):
    last = s + 1 == STEPS
    outs = [shape(USER_ROWS)] * 3 if last else [shape(PART, BF16), shape(3 * USER_ROWS)]
    return kernel_call(
        functools.partial(user_body, s, len(state)),
        outs,
        [SMEM, SMEM] + [VMEM] * (2 + len(state)) + [ANY] * (len(pieces) + len(later)),
        scratch=fetch_scratch(2 * ITEM_ROWS),
        flops=4 * ITEM_TILES * USER_ROWS * TILE * K,
        moved=5 << 20,
    )(me, counts, dense, rows, *state, *pieces, *later)


def item_body(s, states, me_ref, own_ref, other_ref, *rest):
    state_refs, pieces = rest[:states], rest[states : states + len(DISTANCES)]
    *outs, held, sems = rest[states + len(DISTANCES) :]
    copies = fetched(pieces, 2 * ITEM_ROWS, held, sems)
    lane = lax.broadcasted_iota(jnp.int32, (COUNT_ROWS, K), 1)
    weighted = [jnp.zeros((K, K), F32) for _ in range(2)]
    for i, copy in enumerate(copies):
        copy.wait()
        for swap in range(2):
            top = swap * PART
            counts = held[i, top + USER_ROWS : top + PART].astype(F32)
            for u in range(USER_TILES):
                users = held[i, top + u * TILE : top + (u + 1) * TILE]
                gram = lax.dot_general(
                    users, users, (((0,), (0,)), ((), ())), preferred_element_type=F32
                )
                for h in range(2):
                    at = u * ITEM_TILES + me_ref[0] * 2 + h
                    many = jnp.sum(jnp.where(lane == at, counts, 0.0), axis=1, keepdims=True)
                    weighted[h] = weighted[h] + many[0:1] * gram
    fac, first, second = loaded(state_refs)
    rows = fac.astype(BF16)
    parts = []
    for h in range(2):
        high = weighted[h].astype(BF16)
        low = (weighted[h] - high.astype(F32)).astype(BF16)
        mine = rows[h * TILE : (h + 1) * TILE]
        parts.append(
            jnp.dot(mine, high, preferred_element_type=F32)
            + jnp.dot(mine, low, preferred_element_type=F32)
        )
    total = jnp.concatenate(parts, axis=0) - (
        own_ref[:ITEM_ROWS].astype(F32) + other_ref[...].astype(F32)
    )
    grad = GRAD_SCALE * total + DECAY_REG * fac
    fac, first, second = adam_update(fac, first, second, grad)
    stored(outs, (fac, first, second))


def item_step(s, me, own, other, state, pieces):
    last = s + 1 == STEPS
    outs = [shape(ITEM_ROWS)] * 3 if last else [shape(3 * ITEM_ROWS)]
    return kernel_call(
        functools.partial(item_body, s, len(state)),
        outs,
        [SMEM] + [VMEM] * (2 + len(state)) + [ANY] * len(pieces),
        scratch=fetch_scratch(2 * PART),
        flops=2 * 32 * TILE * K * K,
        moved=4 << 20,
    )(me, own, other, *state, *pieces)


def after(value, *others):
    return lax.optimization_barrier((value, *others))[0]


def per_device(
    user_factors,
    user_m,
    user_v,
    item_factors,
    item_m,
    item_v,
    ratings,
    user_tiles,
    item_tiles,
    tile_counts,
):
    strata = lax.axis_size("blk")
    forward = [(z * RING + y, z * RING + (y + 1) % RING) for z in range(2) for y in range(RING)]
    backward = [(target, source) for source, target in forward]
    across = [(n, (n + RING) % (2 * RING)) for n in range(2 * RING)]
    rings = [[z * RING + y for y in range(RING)] for z in range(2)]

    earlier = [(b, (b - 1) % strata) for b in range(strata)]
    me = lax.axis_index("narrow").reshape(1).astype(jnp.int32)
    users_at, items_at = user_tiles.reshape(-1), item_tiles.reshape(-1)
    live = tile_counts.reshape(-1)
    first, rows, counts = opening(users_at, items_at, live, user_factors, item_factors)
    dense = dense_ratings(0, users_at, items_at, live, ratings, first)
    user_state = (user_factors, user_m, user_v)
    item_state = (item_factors, item_m, item_v)
    for s in range(STEPS):
        load = packed(first, lax.ppermute(first, "narrow", across))
        partial = lax.psum_scatter(
            rating_part(me, first, dense),
            "narrow",
            scatter_dimension=0,
            tiled=True,
            axis_index_groups=rings,
        )
        pieces = [load]
        up = down = load
        for step in range(3):
            up = lax.ppermute(up, "narrow", forward)
            down = lax.ppermute(down, "narrow", backward)
            pieces += [up, down]
            if step == 1 and s + 1 < STEPS:
                dense_next = dense_ratings(s + 1, users_at, items_at, live, ratings, pieces[1])
                up = after(up, dense_next)
            if step == (1 if s > 0 else 2):
                ready = after(partial[ITEM_ROWS:], up, down)
                other = lax.ppermute(ready, "narrow", across)
        pieces.append(lax.ppermute(after(up, other) if s > 0 else up, "narrow", forward))
        item_state = item_step(s, me, partial, other, item_state, pieces)
        if s + 1 < STEPS:
            moved = lax.ppermute(item_state[0], "blk", earlier)
            part, *user_state = user_step(
                s, me, counts, dense, rows, user_state, pieces, item_state
            )
            first = joined(part, moved)
            item_state = [moved]
            dense = dense_next
        else:
            user_state = user_step(s, me, counts, dense, rows, user_state, pieces, [])
    return (*user_state, *item_state)


def solution(mesh):
    return jax.shard_map(
        per_device,
        mesh=mesh,
        in_specs=(
            P(("blk", "narrow"), None),
            P(("blk", "narrow"), None),
            P(("blk", "narrow"), None),
            P(("blk", "narrow"), None),
            P(("blk", "narrow"), None),
            P(("blk", "narrow"), None),
            P("blk", "narrow", None, None, None, None),
            P("blk", "narrow", None, None),
            P("blk", "narrow", None, None),
            P("blk", "narrow", None),
        ),
        out_specs=(
            P(("blk", "narrow"), None),
            P(("blk", "narrow"), None),
            P(("blk", "narrow"), None),
            P(("blk", "narrow"), None),
            P(("blk", "narrow"), None),
            P(("blk", "narrow"), None),
        ),
        check_vma=False,
    )
```

```python
import functools

import jax
import jax.numpy as jnp
from jax import lax
from jax.experimental import pallas as pl
from jax.experimental.pallas import tpu as pltpu
from jax.sharding import PartitionSpec as P

K = 128
TILE = 128
MAXT = 36
STEPS = 3
RING = 8
USER_ROWS = 256
ITEM_ROWS = 256
USER_TILES = 2
ITEM_TILES = 32
COUNT_ROWS = 16
PART = USER_ROWS + COUNT_ROWS
PAIRS = USER_TILES * ITEM_TILES
DISTANCES = (0, -1, 1, -2, 2, -3, 3, -4)


LEARN_RATE = 0.01
BETA_ONE = 0.8
BETA_TWO = 0.95
ADAM_EPS = 1e-08
DECAY_REG = 0.05
GRAD_SCALE = 0.03125

VMEM = pl.BlockSpec(memory_space=pltpu.VMEM)
SMEM = pl.BlockSpec(memory_space=pltpu.SMEM)
ANY = pl.BlockSpec(memory_space=pl.ANY)
F32 = jnp.float32
BF16 = jnp.bfloat16


def shape(rows, dtype=F32):
    return jax.ShapeDtypeStruct((rows, K), dtype)


def adam_update(param, first, second, grad):
    first = BETA_ONE * first + (1.0 - BETA_ONE) * grad
    second = BETA_TWO * second + (1.0 - BETA_TWO) * grad * grad
    return (param - LEARN_RATE * first / (jnp.sqrt(second) + ADAM_EPS), first, second)


def kernel_call(body, outs, in_specs, out_specs=None, scratch=(), flops=0, moved=1 << 20):
    return pl.pallas_call(
        body,
        out_shape=outs,
        in_specs=in_specs,
        out_specs=out_specs or jax.tree.map(lambda _: VMEM, outs),
        scratch_shapes=list(scratch),
        cost_estimate=pl.CostEstimate(flops=flops, bytes_accessed=moved, transcendentals=0),
        compiler_params=pltpu.CompilerParams(vmem_limit_bytes=60 << 20),
    )


def loaded(refs):
    if len(refs) == 3:
        return [ref[...] for ref in refs]
    return [refs[0][i * 256 : (i + 1) * 256] for i in range(3)]


def stored(refs, values):
    if len(refs) == 3:
        for ref, value in zip(refs, values):
            ref[...] = value
    else:
        for i, value in enumerate(values):
            refs[0][i * 256 : (i + 1) * 256] = value


def owned_tile(me, swap, place, half):
    plane = me // RING
    plane = 1 - plane if swap else plane
    return (plane * RING + place) * 2 + half


def opening_body(users_at, items_at, live, users, items, first_out, rows_out, counts_out):
    lane = lax.broadcasted_iota(jnp.int32, (COUNT_ROWS, K), 1)

    def clear(i, carry):
        counts_out[i] = 0.0
        return carry

    lax.fori_loop(0, STEPS * PAIRS, clear, 0)
    for s in range(STEPS):

        def add(t, row):
            pair = users_at[0, 0, s, t] * ITEM_TILES + items_at[0, 0, s, t]
            counts_out[s * PAIRS + pair] = counts_out[s * PAIRS + pair] + 1.0
            return row + jnp.where(lane == pair, 1.0, 0.0)

        row = lax.fori_loop(0, live[0, 0, s], add, jnp.zeros((COUNT_ROWS, K), F32)).astype(BF16)
        if s == 0:
            first_out[USER_ROWS:PART] = row
        rows_out[s * COUNT_ROWS : (s + 1) * COUNT_ROWS] = row
    first_out[:USER_ROWS] = users[...].astype(BF16)
    first_out[PART:] = items[...].astype(BF16)


def opening(users_at, items_at, live, users, items):
    return kernel_call(
        opening_body,
        (
            shape(PART + ITEM_ROWS, BF16),
            shape(STEPS * COUNT_ROWS, BF16),
            jax.ShapeDtypeStruct((STEPS * PAIRS,), F32),
        ),
        [SMEM, SMEM, SMEM, VMEM, VMEM],
        (VMEM, VMEM, SMEM),
    )(users_at, items_at, live, users, items)


def joined_body(part, state, out):
    out[:PART] = part[...]
    out[PART:] = state[:ITEM_ROWS].astype(BF16)


def joined(part, state):
    return kernel_call(joined_body, shape(PART + ITEM_ROWS, BF16), [VMEM, VMEM])(part, state)


def packed_body(own, other, out):
    out[:ITEM_ROWS] = own[PART:]
    out[ITEM_ROWS : 2 * ITEM_ROWS] = other[PART:]
    out[2 * ITEM_ROWS : 2 * ITEM_ROWS + PART] = own[:PART]
    out[2 * ITEM_ROWS + PART :] = other[:PART]


def packed(own, other):
    return kernel_call(packed_body, shape(2 * (ITEM_ROWS + PART), BF16), [VMEM, VMEM])(own, other)


def dense_body(s, users_at, items_at, live, ratings, *rest):
    out_ref, total, tiles, sem = rest[-4:]
    fetch = pltpu.make_async_copy(ratings.at[0, 0, s], tiles, sem)
    fetch.start()
    total[...] = jnp.zeros_like(total)
    fetch.wait()

    def add(t, carry):
        slot = items_at[0, 0, s, t] * USER_TILES + users_at[0, 0, s, t]
        row = pl.multiple_of(slot * TILE, TILE)
        total[pl.ds(row, TILE), :] += tiles[t].astype(F32)
        return carry

    lax.fori_loop(0, live[0, 0, s], add, 0)
    out_ref[...] = total[...].astype(BF16)


def dense_ratings(s, users_at, items_at, live, ratings, *later):
    rows = ITEM_TILES * USER_ROWS
    return kernel_call(
        functools.partial(dense_body, s),
        shape(rows, BF16),
        [SMEM, SMEM, SMEM, ANY] + [ANY] * len(later),
        scratch=[
            pltpu.VMEM((rows, TILE), F32),
            pltpu.VMEM((MAXT, TILE, TILE), BF16),
            pltpu.SemaphoreType.DMA,
        ],
        moved=10 << 20,
    )(users_at, items_at, live, ratings, *later)


def rating_part_body(me_ref, users_ref, dense_ref, out_ref):
    users = users_ref[:USER_ROWS]
    for k in range(ITEM_TILES):
        tile = owned_tile(me_ref[0], k // 2 % 2, k // 4, k % 2)
        row = pl.multiple_of(tile * USER_ROWS, USER_ROWS)
        part = lax.dot_general(
            dense_ref[pl.ds(row, USER_ROWS), :],
            users,
            (((0,), (0,)), ((), ())),
            preferred_element_type=F32,
        )
        out_ref[k * TILE : (k + 1) * TILE] = part.astype(BF16)


def rating_part(me, users, dense):
    return kernel_call(
        rating_part_body,
        shape(ITEM_TILES * TILE, BF16),
        [SMEM, VMEM, VMEM],
        flops=2 * ITEM_TILES * USER_ROWS * TILE * K,
        moved=3 << 20,
    )(me, users, dense)


def fetched(pieces, top, held, sems):
    rows = held.shape[1]
    copies = [
        pltpu.make_async_copy(piece.at[pl.ds(top, rows)], held.at[i], sems.at[i])
        for i, piece in enumerate(pieces)
    ]
    for copy in copies:
        copy.start()
    return copies


def fetch_scratch(rows):
    count = len(DISTANCES)
    return [pltpu.VMEM((count, rows, K), BF16), pltpu.SemaphoreType.DMA((count,))]


def user_body(s, states, me_ref, counts_ref, dense_ref, rows_ref, *rest):
    state_refs, pieces = rest[:states], rest[states : states + len(DISTANCES)]
    *outs, held, sems = rest[states + len(DISTANCES) :]
    outs = outs[-3:] if s + 1 == STEPS else outs[-2:]
    copies = fetched(pieces, 0, held, sems)
    fac, first, second = loaded(state_refs)
    users = fac.astype(BF16)
    total = jnp.zeros((USER_ROWS, K), F32)
    upper = lax.broadcasted_iota(jnp.int32, (USER_ROWS, TILE), 0) < TILE
    me = me_ref[0]
    for i, distance in enumerate(DISTANCES):
        copies[i].wait()
        place = (me % RING + distance + RING) % RING
        for swap in range(2):
            rows = held[i, swap * ITEM_ROWS : (swap + 1) * ITEM_ROWS]
            predicted = lax.dot_general(
                users, rows, (((1,), (1,)), ((), ())), preferred_element_type=F32
            )
            errors = []
            for h in range(2):
                tile = owned_tile(me, swap, place, h)
                row = pl.multiple_of(tile * USER_ROWS, USER_ROWS)
                at = s * PAIRS + tile
                many = jnp.where(upper, counts_ref[at], counts_ref[at + ITEM_TILES])
                ratings = dense_ref[pl.ds(row, USER_ROWS), :].astype(F32)
                errors.append(
                    (predicted[:, h * TILE : (h + 1) * TILE] * many - ratings).astype(BF16)
                )
            total += jnp.dot(
                jnp.concatenate(errors, axis=1), rows, preferred_element_type=F32
            )
    grad = GRAD_SCALE * total + DECAY_REG * fac
    fac, first, second = adam_update(fac, first, second, grad)
    if s + 1 < STEPS:
        part_out, *outs = outs
        part_out[:USER_ROWS] = fac.astype(BF16)
        part_out[USER_ROWS:] = rows_ref[(s + 1) * COUNT_ROWS : (s + 2) * COUNT_ROWS]
    stored(outs, (fac, first, second))


def user_step(s, me, counts, dense, rows, state, pieces, later):
    last = s + 1 == STEPS
    outs = [shape(USER_ROWS)] * 3 if last else [shape(PART, BF16), shape(3 * USER_ROWS)]
    return kernel_call(
        functools.partial(user_body, s, len(state)),
        outs,
        [SMEM, SMEM] + [VMEM] * (2 + len(state)) + [ANY] * (len(pieces) + len(later)),
        scratch=fetch_scratch(2 * ITEM_ROWS),
        flops=4 * ITEM_TILES * USER_ROWS * TILE * K,
        moved=5 << 20,
    )(me, counts, dense, rows, *state, *pieces, *later)


def item_body(s, states, me_ref, own_ref, other_ref, *rest):
    state_refs, pieces = rest[:states], rest[states : states + len(DISTANCES)]
    *outs, held, sems = rest[states + len(DISTANCES) :]
    copies = fetched(pieces, 2 * ITEM_ROWS, held, sems)
    lane = lax.broadcasted_iota(jnp.int32, (COUNT_ROWS, K), 1)
    weighted = [jnp.zeros((K, K), F32) for _ in range(2)]
    for i, copy in enumerate(copies):
        copy.wait()
        for swap in range(2):
            top = swap * PART
            counts = held[i, top + USER_ROWS : top + PART].astype(F32)
            for u in range(USER_TILES):
                users = held[i, top + u * TILE : top + (u + 1) * TILE]
                gram = lax.dot_general(
                    users, users, (((0,), (0,)), ((), ())), preferred_element_type=F32
                )
                for h in range(2):
                    at = u * ITEM_TILES + me_ref[0] * 2 + h
                    many = jnp.sum(jnp.where(lane == at, counts, 0.0), axis=1, keepdims=True)
                    weighted[h] = weighted[h] + many[0:1] * gram
    fac, first, second = loaded(state_refs)
    rows = fac.astype(BF16)
    parts = []
    for h in range(2):
        high = weighted[h].astype(BF16)
        low = (weighted[h] - high.astype(F32)).astype(BF16)
        mine = rows[h * TILE : (h + 1) * TILE]
        parts.append(
            jnp.dot(mine, high, preferred_element_type=F32)
            + jnp.dot(mine, low, preferred_element_type=F32)
        )
    total = jnp.concatenate(parts, axis=0) - (
        own_ref[:ITEM_ROWS].astype(F32) + other_ref[...].astype(F32)
    )
    grad = GRAD_SCALE * total + DECAY_REG * fac
    fac, first, second = adam_update(fac, first, second, grad)
    stored(outs, (fac, first, second))


def item_step(s, me, own, other, state, pieces):
    last = s + 1 == STEPS
    outs = [shape(ITEM_ROWS)] * 3 if last else [shape(3 * ITEM_ROWS)]
    return kernel_call(
        functools.partial(item_body, s, len(state)),
        outs,
        [SMEM] + [VMEM] * (2 + len(state)) + [ANY] * len(pieces),
        scratch=fetch_scratch(2 * PART),
        flops=2 * 32 * TILE * K * K,
        moved=4 << 20,
    )(me, own, other, *state, *pieces)


def after(value, *others):
    return lax.optimization_barrier((value, *others))[0]


def per_device(
    user_factors,
    user_m,
    user_v,
    item_factors,
    item_m,
    item_v,
    ratings,
    user_tiles,
    item_tiles,
    tile_counts,
):
    strata = lax.axis_size("blk")
    forward = [(z * RING + y, z * RING + (y + 1) % RING) for z in range(2) for y in range(RING)]
    backward = [(target, source) for source, target in forward]
    across = [(n, (n + RING) % (2 * RING)) for n in range(2 * RING)]
    rings = [[z * RING + y for y in range(RING)] for z in range(2)]

    earlier = [(b, (b - 1) % strata) for b in range(strata)]
    me = lax.axis_index("narrow").reshape(1).astype(jnp.int32)
    users_at, items_at, live = user_tiles, item_tiles, tile_counts
    first, rows, counts = opening(users_at, items_at, live, user_factors, item_factors)
    dense = dense_ratings(0, users_at, items_at, live, ratings, first)
    user_state = (user_factors, user_m, user_v)
    item_state = (item_factors, item_m, item_v)
    for s in range(STEPS):
        load = packed(first, lax.ppermute(first, "narrow", across))
        partial = lax.psum_scatter(
            rating_part(me, first, dense),
            "narrow",
            scatter_dimension=0,
            tiled=True,
            axis_index_groups=rings,
        )
        pieces = [load]
        up = down = load
        for step in range(3):
            up = lax.ppermute(up, "narrow", forward)
            down = lax.ppermute(down, "narrow", backward)
            pieces += [up, down]
            if step == 1 and s + 1 < STEPS:
                dense_next = dense_ratings(s + 1, users_at, items_at, live, ratings, pieces[1])
                up = after(up, dense_next)
            if step == 2:
                ready = after(partial[ITEM_ROWS:], up, down)
                other = lax.ppermute(ready, "narrow", across)
        pieces.append(lax.ppermute(after(up, ready), "narrow", forward))
        item_state = item_step(s, me, partial, other, item_state, pieces)
        if s + 1 < STEPS:
            moved = lax.ppermute(item_state[0], "blk", earlier)
            part, *user_state = user_step(
                s, me, counts, dense, rows, user_state, pieces, item_state
            )
            first = joined(part, moved)
            item_state = [moved]
            dense = dense_next
        else:
            user_state = user_step(s, me, counts, dense, rows, user_state, pieces, [])
    return (*user_state, *item_state)


def solution(mesh):
    return jax.shard_map(
        per_device,
        mesh=mesh,
        in_specs=(
            P(("blk", "narrow"), None),
            P(("blk", "narrow"), None),
            P(("blk", "narrow"), None),
            P(("blk", "narrow"), None),
            P(("blk", "narrow"), None),
            P(("blk", "narrow"), None),
            P("blk", "narrow", None, None, None, None),
            P("blk", "narrow", None, None),
            P("blk", "narrow", None, None),
            P("blk", "narrow", None),
        ),
        out_specs=(
            P(("blk", "narrow"), None),
            P(("blk", "narrow"), None),
            P(("blk", "narrow"), None),
            P(("blk", "narrow"), None),
            P(("blk", "narrow"), None),
            P(("blk", "narrow"), None),
        ),
        check_vma=False,
    )
```

```python
import functools

import jax
import jax.numpy as jnp
from jax import lax
from jax.experimental import pallas as pl
from jax.experimental.pallas import tpu as pltpu
from jax.sharding import PartitionSpec as P

K = 128
TILE = 128
MAXT = 36
STEPS = 3
RING = 8
USER_ROWS = 256
ITEM_ROWS = 256
USER_TILES = 2
ITEM_TILES = 32
COUNT_ROWS = 16
PART = USER_ROWS + COUNT_ROWS
PAIRS = USER_TILES * ITEM_TILES
DISTANCES = (0, -1, 1, -2, 2, -3, 3, -4)


LEARN_RATE = 0.01
BETA_ONE = 0.8
BETA_TWO = 0.95
ADAM_EPS = 1e-08
DECAY_REG = 0.05
GRAD_SCALE = 0.03125

VMEM = pl.BlockSpec(memory_space=pltpu.VMEM)
SMEM = pl.BlockSpec(memory_space=pltpu.SMEM)
ANY = pl.BlockSpec(memory_space=pl.ANY)
F32 = jnp.float32
BF16 = jnp.bfloat16


def shape(rows, dtype=F32):
    return jax.ShapeDtypeStruct((rows, K), dtype)


def adam_update(param, first, second, grad):
    first = BETA_ONE * first + (1.0 - BETA_ONE) * grad
    second = BETA_TWO * second + (1.0 - BETA_TWO) * grad * grad
    return (param - LEARN_RATE * first / (jnp.sqrt(second) + ADAM_EPS), first, second)


def kernel_call(body, outs, in_specs, out_specs=None, scratch=(), flops=0, moved=1 << 20):
    return pl.pallas_call(
        body,
        out_shape=outs,
        in_specs=in_specs,
        out_specs=out_specs or jax.tree.map(lambda _: VMEM, outs),
        scratch_shapes=list(scratch),
        cost_estimate=pl.CostEstimate(flops=flops, bytes_accessed=moved, transcendentals=0),
        compiler_params=pltpu.CompilerParams(vmem_limit_bytes=40 << 20),
    )


def loaded(refs):
    if len(refs) == 3:
        return [ref[...] for ref in refs]
    return [refs[0][i * 256 : (i + 1) * 256] for i in range(3)]


def stored(refs, values):
    if len(refs) == 3:
        for ref, value in zip(refs, values):
            ref[...] = value
    else:
        for i, value in enumerate(values):
            refs[0][i * 256 : (i + 1) * 256] = value


def owned_tile(me, swap, place, half):
    plane = me // RING
    plane = 1 - plane if swap else plane
    return (plane * RING + place) * 2 + half


def opening_body(users_at, items_at, live, users, items, first_out, rows_out, counts_out):
    lane = lax.broadcasted_iota(jnp.int32, (COUNT_ROWS, K), 1)

    def clear(i, carry):
        counts_out[i] = 0.0
        return carry

    lax.fori_loop(0, STEPS * PAIRS, clear, 0)
    for s in range(STEPS):

        def add(t, row):
            pair = users_at[s * MAXT + t] * ITEM_TILES + items_at[s * MAXT + t]
            counts_out[s * PAIRS + pair] = counts_out[s * PAIRS + pair] + 1.0
            return row + jnp.where(lane == pair, 1.0, 0.0)

        row = lax.fori_loop(0, live[s], add, jnp.zeros((COUNT_ROWS, K), F32)).astype(BF16)
        if s == 0:
            first_out[USER_ROWS:PART] = row
        rows_out[s * COUNT_ROWS : (s + 1) * COUNT_ROWS] = row
    first_out[:USER_ROWS] = users[...].astype(BF16)
    first_out[PART:] = items[...].astype(BF16)


def opening(users_at, items_at, live, users, items):
    return kernel_call(
        opening_body,
        (
            shape(PART + ITEM_ROWS, BF16),
            shape(STEPS * COUNT_ROWS, BF16),
            jax.ShapeDtypeStruct((STEPS * PAIRS,), F32),
        ),
        [SMEM, SMEM, SMEM, VMEM, VMEM],
        (VMEM, VMEM, SMEM),
    )(users_at, items_at, live, users, items)


def joined_body(part, state, out):
    out[:PART] = part[...]
    out[PART:] = state[:ITEM_ROWS].astype(BF16)


def joined(part, state):
    return kernel_call(joined_body, shape(PART + ITEM_ROWS, BF16), [VMEM, VMEM])(part, state)


def packed_body(own, other, out):
    out[:ITEM_ROWS] = own[PART:]
    out[ITEM_ROWS : 2 * ITEM_ROWS] = other[PART:]
    out[2 * ITEM_ROWS : 2 * ITEM_ROWS + PART] = own[:PART]
    out[2 * ITEM_ROWS + PART :] = other[:PART]


def packed(own, other):
    return kernel_call(packed_body, shape(2 * (ITEM_ROWS + PART), BF16), [VMEM, VMEM])(own, other)


def dense_body(s, users_at, items_at, live, ratings, *rest):
    out_ref, total, tiles, sem = rest[-4:]
    fetch = pltpu.make_async_copy(ratings.at[0, 0, s], tiles, sem)
    fetch.start()
    total[...] = jnp.zeros_like(total)
    fetch.wait()

    def add(t, carry):
        slot = items_at[s * MAXT + t] * USER_TILES + users_at[s * MAXT + t]
        row = pl.multiple_of(slot * TILE, TILE)
        total[pl.ds(row, TILE), :] += tiles[t].astype(F32)
        return carry

    lax.fori_loop(0, live[s], add, 0)
    out_ref[...] = total[...].astype(BF16)


def dense_ratings(s, users_at, items_at, live, ratings, *later):
    rows = ITEM_TILES * USER_ROWS
    return kernel_call(
        functools.partial(dense_body, s),
        shape(rows, BF16),
        [SMEM, SMEM, SMEM, ANY] + [ANY] * len(later),
        scratch=[
            pltpu.VMEM((rows, TILE), F32),
            pltpu.VMEM((MAXT, TILE, TILE), BF16),
            pltpu.SemaphoreType.DMA,
        ],
        moved=10 << 20,
    )(users_at, items_at, live, ratings, *later)


def rating_part_body(me_ref, users_ref, dense_ref, out_ref):
    users = users_ref[:USER_ROWS]
    for k in range(ITEM_TILES):
        tile = owned_tile(me_ref[0], k // 2 % 2, k // 4, k % 2)
        row = pl.multiple_of(tile * USER_ROWS, USER_ROWS)
        part = lax.dot_general(
            dense_ref[pl.ds(row, USER_ROWS), :],
            users,
            (((0,), (0,)), ((), ())),
            preferred_element_type=F32,
        )
        out_ref[k * TILE : (k + 1) * TILE] = part.astype(BF16)


def rating_part(me, users, dense):
    return kernel_call(
        rating_part_body,
        shape(ITEM_TILES * TILE, BF16),
        [SMEM, VMEM, VMEM],
        flops=2 * ITEM_TILES * USER_ROWS * TILE * K,
        moved=40 << 20,
    )(me, users, dense)


def user_body(s, states, me_ref, counts_ref, dense_ref, rows_ref, *rest):
    state_refs, pieces = rest[:states], rest[states : states + len(DISTANCES)]
    outs = rest[-3:] if s + 1 == STEPS else rest[-2:]
    fac, first, second = loaded(state_refs)
    users = fac.astype(BF16)
    total = jnp.zeros((USER_ROWS, K), F32)
    upper = lax.broadcasted_iota(jnp.int32, (USER_ROWS, TILE), 0) < TILE
    me = me_ref[0]
    for piece, distance in zip(pieces, DISTANCES):
        place = (me % RING + distance * me_ref[1] + RING) % RING
        for swap in range(2):
            rows = piece[swap * ITEM_ROWS : (swap + 1) * ITEM_ROWS]
            predicted = lax.dot_general(
                users, rows, (((1,), (1,)), ((), ())), preferred_element_type=F32
            )
            errors = []
            for h in range(2):
                tile = owned_tile(me, swap, place, h)
                row = pl.multiple_of(tile * USER_ROWS, USER_ROWS)
                at = s * PAIRS + tile
                many = jnp.where(upper, counts_ref[at], counts_ref[at + ITEM_TILES])
                ratings = dense_ref[pl.ds(row, USER_ROWS), :].astype(F32)
                errors.append(
                    (predicted[:, h * TILE : (h + 1) * TILE] * many - ratings).astype(BF16)
                )
            total += jnp.dot(
                jnp.concatenate(errors, axis=1), rows, preferred_element_type=F32
            )
    grad = GRAD_SCALE * total + DECAY_REG * fac
    fac, first, second = adam_update(fac, first, second, grad)
    if s + 1 < STEPS:
        part_out, *outs = outs
        part_out[:USER_ROWS] = fac.astype(BF16)
        part_out[USER_ROWS:] = rows_ref[(s + 1) * COUNT_ROWS : (s + 2) * COUNT_ROWS]
    stored(outs, (fac, first, second))


def user_step(s, me, counts, dense, rows, state, pieces, later):
    last = s + 1 == STEPS
    outs = [shape(USER_ROWS)] * 3 if last else [shape(PART, BF16), shape(3 * USER_ROWS)]
    return kernel_call(
        functools.partial(user_body, s, len(state)),
        outs,
        [SMEM, SMEM] + [VMEM] * (2 + len(state) + len(pieces)) + [ANY] * len(later),
        flops=4 * ITEM_TILES * USER_ROWS * TILE * K,
        moved=5 << 20,
    )(me, counts, dense, rows, *state, *pieces, *later)


def item_body(s, states, me_ref, own_ref, other_ref, *rest):
    state_refs, pieces = rest[:states], rest[states : states + len(DISTANCES)]
    outs = rest[states + len(DISTANCES) :]
    lane = lax.broadcasted_iota(jnp.int32, (COUNT_ROWS, K), 1)
    weighted = [jnp.zeros((K, K), F32) for _ in range(2)]
    for piece in pieces:
        for swap in range(2):
            top = 2 * ITEM_ROWS + swap * PART
            counts = piece[top + USER_ROWS : top + PART].astype(F32)
            for u in range(USER_TILES):
                users = piece[top + u * TILE : top + (u + 1) * TILE]
                gram = lax.dot_general(
                    users, users, (((0,), (0,)), ((), ())), preferred_element_type=F32
                )
                for h in range(2):
                    at = u * ITEM_TILES + me_ref[0] * 2 + h
                    many = jnp.sum(jnp.where(lane == at, counts, 0.0), axis=1, keepdims=True)
                    weighted[h] = weighted[h] + many[0:1] * gram
    fac, first, second = loaded(state_refs)
    rows = fac.astype(BF16)
    parts = []
    for h in range(2):
        high = weighted[h].astype(BF16)
        low = (weighted[h] - high.astype(F32)).astype(BF16)
        mine = rows[h * TILE : (h + 1) * TILE]
        parts.append(
            jnp.dot(mine, high, preferred_element_type=F32)
            + jnp.dot(mine, low, preferred_element_type=F32)
        )
    total = jnp.concatenate(parts, axis=0) - (
        own_ref[:ITEM_ROWS].astype(F32) + other_ref[...].astype(F32)
    )
    grad = GRAD_SCALE * total + DECAY_REG * fac
    fac, first, second = adam_update(fac, first, second, grad)
    stored(outs, (fac, first, second))


def item_step(s, me, own, other, state, pieces):
    last = s + 1 == STEPS
    outs = [shape(ITEM_ROWS)] * 3 if last else [shape(3 * ITEM_ROWS)]
    return kernel_call(
        functools.partial(item_body, s, len(state)),
        outs,
        [SMEM] + [VMEM] * (2 + len(state) + len(pieces)),
        flops=2 * 32 * TILE * K * K,
        moved=4 << 20,
    )(me, own, other, *state, *pieces)


def after(value, *others):
    return lax.optimization_barrier((value, *others))[0]


def per_device(
    user_factors,
    user_m,
    user_v,
    item_factors,
    item_m,
    item_v,
    ratings,
    user_tiles,
    item_tiles,
    tile_counts,
):
    strata = lax.axis_size("blk")
    members = 2 * RING

    def ring_route(step):
        return [
            (b * members + n, b * members + n // RING * RING + (n + (-step if b % 2 else step)) % RING)
            for b in range(strata)
            for n in range(members)
        ]

    forward, backward = ring_route(1), ring_route(-1)
    across = [(n, (n + RING) % (2 * RING)) for n in range(2 * RING)]
    rings = [[z * RING + y for y in range(RING)] for z in range(2)]

    earlier = [(b, (b - 1) % strata) for b in range(strata)]
    way = 1 - 2 * (lax.axis_index("blk") % 2)
    me = jnp.stack([lax.axis_index("narrow"), way]).astype(jnp.int32)
    users_at, items_at = user_tiles.reshape(-1), item_tiles.reshape(-1)
    live = tile_counts.reshape(-1)
    first, rows, counts = opening(users_at, items_at, live, user_factors, item_factors)
    dense = dense_ratings(0, users_at, items_at, live, ratings, first)
    user_state = (user_factors, user_m, user_v)
    item_state = (item_factors, item_m, item_v)
    for s in range(STEPS):
        load = packed(first, lax.ppermute(first, "narrow", across))
        partial = lax.psum_scatter(
            rating_part(me, first, dense),
            "narrow",
            scatter_dimension=0,
            tiled=True,
            axis_index_groups=rings,
        )
        pieces = [load]
        up = down = load
        for step in range(3):
            up = lax.ppermute(up, ("blk", "narrow"), forward)
            down = lax.ppermute(down, ("blk", "narrow"), backward)
            pieces += [up, down]
            if step == 1 and s + 1 < STEPS:
                dense_next = dense_ratings(s + 1, users_at, items_at, live, ratings, pieces[1])
                up = after(up, dense_next)
            if step == 2:
                ready = after(partial[ITEM_ROWS:], up, down)
                other = lax.ppermute(ready, "narrow", across)
        pieces.append(lax.ppermute(after(up, ready), ("blk", "narrow"), forward))
        item_state = item_step(s, me, partial, other, item_state, pieces)
        if s + 1 < STEPS:
            moved = lax.ppermute(item_state[0], "blk", earlier)
            part, *user_state = user_step(
                s, me, counts, dense, rows, user_state, pieces, item_state
            )
            first = joined(part, moved)
            item_state = [moved]
            dense = dense_next
        else:
            user_state = user_step(s, me, counts, dense, rows, user_state, pieces, [])
    return (*user_state, *item_state)


def solution(mesh):
    return jax.shard_map(
        per_device,
        mesh=mesh,
        in_specs=(
            P(("blk", "narrow"), None),
            P(("blk", "narrow"), None),
            P(("blk", "narrow"), None),
            P(("blk", "narrow"), None),
            P(("blk", "narrow"), None),
            P(("blk", "narrow"), None),
            P("blk", "narrow", None, None, None, None),
            P("blk", "narrow", None, None),
            P("blk", "narrow", None, None),
            P("blk", "narrow", None),
        ),
        out_specs=(
            P(("blk", "narrow"), None),
            P(("blk", "narrow"), None),
            P(("blk", "narrow"), None),
            P(("blk", "narrow"), None),
            P(("blk", "narrow"), None),
            P(("blk", "narrow"), None),
        ),
        check_vma=False,
    )
```

```python
import functools

import jax
import jax.numpy as jnp
from jax import lax
from jax.experimental import pallas as pl
from jax.experimental.pallas import tpu as pltpu
from jax.sharding import PartitionSpec as P

K = 128
TILE = 128
MAXT = 36
STEPS = 3
RING = 8
USER_ROWS = 256
ITEM_ROWS = 256
USER_TILES = 2
ITEM_TILES = 32
COUNT_ROWS = 16
PART = USER_ROWS + COUNT_ROWS
PAIRS = USER_TILES * ITEM_TILES
DISTANCES = (0, -1, 1, -2, 2, -3, 3, -4)


LEARN_RATE = 0.01
BETA_ONE = 0.8
BETA_TWO = 0.95
ADAM_EPS = 1e-08
DECAY_REG = 0.05
GRAD_SCALE = 0.03125

VMEM = pl.BlockSpec(memory_space=pltpu.VMEM)
SMEM = pl.BlockSpec(memory_space=pltpu.SMEM)
ANY = pl.BlockSpec(memory_space=pl.ANY)
F32 = jnp.float32
BF16 = jnp.bfloat16


def shape(rows, dtype=F32):
    return jax.ShapeDtypeStruct((rows, K), dtype)


def adam_update(param, first, second, grad):
    first = BETA_ONE * first + (1.0 - BETA_ONE) * grad
    second = BETA_TWO * second + (1.0 - BETA_TWO) * grad * grad
    return (param - LEARN_RATE * first / (jnp.sqrt(second) + ADAM_EPS), first, second)


def kernel_call(body, outs, in_specs, out_specs=None, scratch=(), flops=0, moved=1 << 20):
    return pl.pallas_call(
        body,
        out_shape=outs,
        in_specs=in_specs,
        out_specs=out_specs or jax.tree.map(lambda _: VMEM, outs),
        scratch_shapes=list(scratch),
        cost_estimate=pl.CostEstimate(flops=flops, bytes_accessed=moved, transcendentals=0),
        compiler_params=pltpu.CompilerParams(vmem_limit_bytes=40 << 20),
    )


def loaded(refs):
    if len(refs) == 3:
        return [ref[...] for ref in refs]
    return [refs[0][i * 256 : (i + 1) * 256] for i in range(3)]


def stored(refs, values):
    if len(refs) == 3:
        for ref, value in zip(refs, values):
            ref[...] = value
    else:
        for i, value in enumerate(values):
            refs[0][i * 256 : (i + 1) * 256] = value


def owned_tile(me, swap, place, half):
    plane = me // RING
    plane = 1 - plane if swap else plane
    return (plane * RING + place) * 2 + half


def opening_body(users_at, items_at, live, users, items, first_out, rows_out, counts_out):
    lane = lax.broadcasted_iota(jnp.int32, (COUNT_ROWS, K), 1)

    def clear(i, carry):
        counts_out[i] = 0.0
        return carry

    lax.fori_loop(0, STEPS * PAIRS, clear, 0)
    for s in range(STEPS):

        def add(t, row):
            pair = users_at[s * MAXT + t] * ITEM_TILES + items_at[s * MAXT + t]
            counts_out[s * PAIRS + pair] = counts_out[s * PAIRS + pair] + 1.0
            return row + jnp.where(lane == pair, 1.0, 0.0)

        row = lax.fori_loop(0, live[s], add, jnp.zeros((COUNT_ROWS, K), F32)).astype(BF16)
        if s == 0:
            first_out[USER_ROWS:PART] = row
        rows_out[s * COUNT_ROWS : (s + 1) * COUNT_ROWS] = row
    first_out[:USER_ROWS] = users[...].astype(BF16)
    first_out[PART:] = items[...].astype(BF16)


def opening(users_at, items_at, live, users, items):
    return kernel_call(
        opening_body,
        (
            shape(PART + ITEM_ROWS, BF16),
            shape(STEPS * COUNT_ROWS, BF16),
            jax.ShapeDtypeStruct((STEPS * PAIRS,), F32),
        ),
        [SMEM, SMEM, SMEM, VMEM, VMEM],
        (VMEM, VMEM, SMEM),
    )(users_at, items_at, live, users, items)


def joined_body(part, state, out):
    out[:PART] = part[...]
    out[PART:] = state[:ITEM_ROWS].astype(BF16)


def joined(part, state):
    return kernel_call(joined_body, shape(PART + ITEM_ROWS, BF16), [VMEM, VMEM])(part, state)


def packed_body(me_ref, both, out):
    plane = me_ref[0] // RING
    for swap in range(2):
        top = pl.multiple_of((1 - plane if swap else plane) * (PART + ITEM_ROWS), 16)
        out[swap * ITEM_ROWS : (swap + 1) * ITEM_ROWS] = both[pl.ds(top + PART, ITEM_ROWS)]
        users = 2 * ITEM_ROWS + swap * PART
        out[users : users + PART] = both[pl.ds(top, PART)]


def packed(me, both):
    return kernel_call(packed_body, shape(2 * (ITEM_ROWS + PART), BF16), [SMEM, VMEM])(me, both)


def dense_body(s, users_at, items_at, live, ratings, *rest):
    out_ref, total, tiles, sem = rest[-4:]
    fetch = pltpu.make_async_copy(ratings.at[0, 0, s], tiles, sem)
    fetch.start()
    total[...] = jnp.zeros_like(total)
    fetch.wait()

    def add(t, carry):
        slot = items_at[s * MAXT + t] * USER_TILES + users_at[s * MAXT + t]
        row = pl.multiple_of(slot * TILE, TILE)
        total[pl.ds(row, TILE), :] += tiles[t].astype(F32)
        return carry

    lax.fori_loop(0, live[s], add, 0)
    out_ref[...] = total[...].astype(BF16)


def dense_ratings(s, users_at, items_at, live, ratings, *later):
    rows = ITEM_TILES * USER_ROWS
    return kernel_call(
        functools.partial(dense_body, s),
        shape(rows, BF16),
        [SMEM, SMEM, SMEM, ANY] + [ANY] * len(later),
        scratch=[
            pltpu.VMEM((rows, TILE), F32),
            pltpu.VMEM((MAXT, TILE, TILE), BF16),
            pltpu.SemaphoreType.DMA,
        ],
        moved=10 << 20,
    )(users_at, items_at, live, ratings, *later)


def rating_part_body(me_ref, users_ref, dense_ref, out_ref):
    users = users_ref[:USER_ROWS]
    for k in range(ITEM_TILES):
        tile = owned_tile(me_ref[0], k // 2 % 2, k // 4, k % 2)
        row = pl.multiple_of(tile * USER_ROWS, USER_ROWS)
        part = lax.dot_general(
            dense_ref[pl.ds(row, USER_ROWS), :],
            users,
            (((0,), (0,)), ((), ())),
            preferred_element_type=F32,
        )
        out_ref[k * TILE : (k + 1) * TILE] = part.astype(BF16)


def rating_part(me, users, dense):
    return kernel_call(
        rating_part_body,
        shape(ITEM_TILES * TILE, BF16),
        [SMEM, VMEM, VMEM],
        flops=2 * ITEM_TILES * USER_ROWS * TILE * K,
        moved=40 << 20,
    )(me, users, dense)


def user_body(s, states, me_ref, counts_ref, dense_ref, rows_ref, *rest):
    state_refs, pieces = rest[:states], rest[states : states + len(DISTANCES)]
    outs = rest[-3:] if s + 1 == STEPS else rest[-2:]
    fac, first, second = loaded(state_refs)
    users = fac.astype(BF16)
    total = jnp.zeros((USER_ROWS, K), F32)
    upper = lax.broadcasted_iota(jnp.int32, (USER_ROWS, TILE), 0) < TILE
    me = me_ref[0]
    for piece, distance in zip(pieces, DISTANCES):
        place = (me % RING + distance * me_ref[1] + RING) % RING
        for swap in range(2):
            rows = piece[swap * ITEM_ROWS : (swap + 1) * ITEM_ROWS]
            predicted = lax.dot_general(
                users, rows, (((1,), (1,)), ((), ())), preferred_element_type=F32
            )
            errors = []
            for h in range(2):
                tile = owned_tile(me, swap, place, h)
                row = pl.multiple_of(tile * USER_ROWS, USER_ROWS)
                at = s * PAIRS + tile
                many = jnp.where(upper, counts_ref[at], counts_ref[at + ITEM_TILES])
                ratings = dense_ref[pl.ds(row, USER_ROWS), :].astype(F32)
                errors.append(
                    (predicted[:, h * TILE : (h + 1) * TILE] * many - ratings).astype(BF16)
                )
            total += jnp.dot(
                jnp.concatenate(errors, axis=1), rows, preferred_element_type=F32
            )
    grad = GRAD_SCALE * total + DECAY_REG * fac
    fac, first, second = adam_update(fac, first, second, grad)
    if s + 1 < STEPS:
        part_out, *outs = outs
        part_out[:USER_ROWS] = fac.astype(BF16)
        part_out[USER_ROWS:] = rows_ref[(s + 1) * COUNT_ROWS : (s + 2) * COUNT_ROWS]
    stored(outs, (fac, first, second))


def user_step(s, me, counts, dense, rows, state, pieces, later):
    last = s + 1 == STEPS
    outs = [shape(USER_ROWS)] * 3 if last else [shape(PART, BF16), shape(3 * USER_ROWS)]
    return kernel_call(
        functools.partial(user_body, s, len(state)),
        outs,
        [SMEM, SMEM] + [VMEM] * (2 + len(state) + len(pieces)) + [ANY] * len(later),
        flops=4 * ITEM_TILES * USER_ROWS * TILE * K,
        moved=5 << 20,
    )(me, counts, dense, rows, *state, *pieces, *later)


def item_body(s, states, me_ref, sums_ref, *rest):
    state_refs, pieces = rest[:states], rest[states : states + len(DISTANCES)]
    outs = rest[states + len(DISTANCES) :]
    lane = lax.broadcasted_iota(jnp.int32, (COUNT_ROWS, K), 1)
    weighted = [jnp.zeros((K, K), F32) for _ in range(2)]
    for piece in pieces:
        for swap in range(2):
            top = 2 * ITEM_ROWS + swap * PART
            counts = piece[top + USER_ROWS : top + PART].astype(F32)
            for u in range(USER_TILES):
                users = piece[top + u * TILE : top + (u + 1) * TILE]
                gram = lax.dot_general(
                    users, users, (((0,), (0,)), ((), ())), preferred_element_type=F32
                )
                for h in range(2):
                    at = u * ITEM_TILES + me_ref[0] * 2 + h
                    many = jnp.sum(jnp.where(lane == at, counts, 0.0), axis=1, keepdims=True)
                    weighted[h] = weighted[h] + many[0:1] * gram
    fac, first, second = loaded(state_refs)
    rows = fac.astype(BF16)
    parts = []
    for h in range(2):
        high = weighted[h].astype(BF16)
        low = (weighted[h] - high.astype(F32)).astype(BF16)
        mine = rows[h * TILE : (h + 1) * TILE]
        parts.append(
            jnp.dot(mine, high, preferred_element_type=F32)
            + jnp.dot(mine, low, preferred_element_type=F32)
        )
    plane = me_ref[0] // RING
    mine_at = pl.multiple_of(plane * 2 * ITEM_ROWS, ITEM_ROWS)
    other_at = pl.multiple_of((1 - plane) * 2 * ITEM_ROWS + ITEM_ROWS, ITEM_ROWS)
    total = jnp.concatenate(parts, axis=0) - (
        sums_ref[pl.ds(mine_at, ITEM_ROWS)].astype(F32)
        + sums_ref[pl.ds(other_at, ITEM_ROWS)].astype(F32)
    )
    grad = GRAD_SCALE * total + DECAY_REG * fac
    fac, first, second = adam_update(fac, first, second, grad)
    stored(outs, (fac, first, second))


def item_step(s, me, sums, state, pieces):
    last = s + 1 == STEPS
    outs = [shape(ITEM_ROWS)] * 3 if last else [shape(3 * ITEM_ROWS)]
    return kernel_call(
        functools.partial(item_body, s, len(state)),
        outs,
        [SMEM] + [VMEM] * (1 + len(state) + len(pieces)),
        flops=2 * 32 * TILE * K * K,
        moved=4 << 20,
    )(me, sums, *state, *pieces)


def after(value, *others):
    return lax.optimization_barrier((value, *others))[0]


def per_device(
    user_factors,
    user_m,
    user_v,
    item_factors,
    item_m,
    item_v,
    ratings,
    user_tiles,
    item_tiles,
    tile_counts,
):
    strata = lax.axis_size("blk")
    members = 2 * RING

    def ring_route(step):
        return [
            (b * members + n, b * members + n // RING * RING + (n + (-step if b % 2 else step)) % RING)
            for b in range(strata)
            for n in range(members)
        ]

    forward, backward = ring_route(1), ring_route(-1)
    facing = [[y, y + RING] for y in range(RING)]

    def both_planes(rows):
        return lax.all_gather(rows, "narrow", axis=0, tiled=True, axis_index_groups=facing)

    rings = [[z * RING + y for y in range(RING)] for z in range(2)]

    earlier = [(b, (b - 1) % strata) for b in range(strata)]
    way = 1 - 2 * (lax.axis_index("blk") % 2)
    me = jnp.stack([lax.axis_index("narrow"), way]).astype(jnp.int32)
    users_at, items_at = user_tiles.reshape(-1), item_tiles.reshape(-1)
    live = tile_counts.reshape(-1)
    first, rows, counts = opening(users_at, items_at, live, user_factors, item_factors)
    dense = dense_ratings(0, users_at, items_at, live, ratings, first)
    user_state = (user_factors, user_m, user_v)
    item_state = (item_factors, item_m, item_v)
    for s in range(STEPS):
        load = packed(me, both_planes(first))
        partial = lax.psum_scatter(
            rating_part(me, first, dense),
            "narrow",
            scatter_dimension=0,
            tiled=True,
            axis_index_groups=rings,
        )
        pieces = [load]
        up = down = load
        for step in range(3):
            up = lax.ppermute(up, ("blk", "narrow"), forward)
            down = lax.ppermute(down, ("blk", "narrow"), backward)
            pieces += [up, down]
            if step == 1 and s + 1 < STEPS:
                dense_next = dense_ratings(s + 1, users_at, items_at, live, ratings, pieces[1])
                up = after(up, dense_next)
            if step == 2:
                sums = both_planes(after(partial, up, down))
        pieces.append(lax.ppermute(up, ("blk", "narrow"), forward))
        item_state = item_step(s, me, sums, item_state, pieces)
        if s + 1 < STEPS:
            moved = lax.ppermute(item_state[0], "blk", earlier)
            part, *user_state = user_step(
                s, me, counts, dense, rows, user_state, pieces, item_state
            )
            first = joined(part, moved)
            item_state = [moved]
            dense = dense_next
        else:
            user_state = user_step(s, me, counts, dense, rows, user_state, pieces, [])
    return (*user_state, *item_state)


def solution(mesh):
    return jax.shard_map(
        per_device,
        mesh=mesh,
        in_specs=(
            P(("blk", "narrow"), None),
            P(("blk", "narrow"), None),
            P(("blk", "narrow"), None),
            P(("blk", "narrow"), None),
            P(("blk", "narrow"), None),
            P(("blk", "narrow"), None),
            P("blk", "narrow", None, None, None, None),
            P("blk", "narrow", None, None),
            P("blk", "narrow", None, None),
            P("blk", "narrow", None),
        ),
        out_specs=(
            P(("blk", "narrow"), None),
            P(("blk", "narrow"), None),
            P(("blk", "narrow"), None),
            P(("blk", "narrow"), None),
            P(("blk", "narrow"), None),
            P(("blk", "narrow"), None),
        ),
        check_vma=False,
    )
```

```python
import functools

import jax
import jax.numpy as jnp
from jax import lax
from jax.experimental import pallas as pl
from jax.experimental.pallas import tpu as pltpu
from jax.sharding import PartitionSpec as P

K = 128
TILE = 128
MAXT = 36
STEPS = 3
USER_ROWS = 256
ITEM_ROWS = 256
USER_TILES = 2
ITEM_TILES = 32
PAIRS = USER_TILES * ITEM_TILES


LEARN_RATE = 0.01
BETA_ONE = 0.8
BETA_TWO = 0.95
ADAM_EPS = 1e-08
DECAY_REG = 0.05
GRAD_SCALE = 0.03125

VMEM = pl.BlockSpec(memory_space=pltpu.VMEM)
SMEM = pl.BlockSpec(memory_space=pltpu.SMEM)
ANY = pl.BlockSpec(memory_space=pl.ANY)
F32 = jnp.float32
BF16 = jnp.bfloat16


def shape(rows, dtype=F32):
    return jax.ShapeDtypeStruct((rows, K), dtype)


def adam_update(param, first, second, grad):
    first = BETA_ONE * first + (1.0 - BETA_ONE) * grad
    second = BETA_TWO * second + (1.0 - BETA_TWO) * grad * grad
    return (param - LEARN_RATE * first / (jnp.sqrt(second) + ADAM_EPS), first, second)


def kernel_call(body, outs, in_specs, out_specs=None, scratch=(), flops=0, moved=1 << 20):
    return pl.pallas_call(
        body,
        out_shape=outs,
        in_specs=in_specs,
        out_specs=out_specs or jax.tree.map(lambda _: VMEM, outs),
        scratch_shapes=list(scratch),
        cost_estimate=pl.CostEstimate(flops=flops, bytes_accessed=moved, transcendentals=0),
        compiler_params=pltpu.CompilerParams(vmem_limit_bytes=40 << 20),
    )


def shifted(block, axis, distance):
    devices = range(lax.axis_size(axis))
    route = [((i - distance) % len(devices), i) for i in devices]
    return lax.ppermute(block, axis, route)


def gathered(rows):
    members = lax.axis_size("narrow")
    copies = jnp.broadcast_to(rows[None], (members,) + rows.shape)
    return lax.all_to_all(copies, "narrow", 0, 0).reshape(members * rows.shape[0], K)


def summed(partial):
    members = lax.axis_size("narrow")
    parts = partial.reshape(members, partial.shape[0] // members, K)
    arrived = lax.all_to_all(parts, "narrow", 0, 0)
    return jnp.sum(arrived.astype(jnp.float32), axis=0)


def dense_body(s, users_at, items_at, live, ratings, *rest):
    out_ref, total, tiles, sem = rest[-4:]
    fetch = pltpu.make_async_copy(ratings.at[0, 0, s], tiles, sem)
    fetch.start()
    total[...] = jnp.zeros_like(total)
    fetch.wait()

    def add(t, carry):
        slot = items_at[s * MAXT + t] * USER_TILES + users_at[s * MAXT + t]
        row = pl.multiple_of(slot * TILE, TILE)
        total[pl.ds(row, TILE), :] += tiles[t].astype(F32)
        return carry

    lax.fori_loop(0, live[s], add, 0)
    out_ref[...] = total[...].astype(BF16)


def dense_ratings(s, users_at, items_at, live, ratings, *later):
    rows = ITEM_TILES * USER_ROWS
    return kernel_call(
        functools.partial(dense_body, s),
        shape(rows, BF16),
        [SMEM, SMEM, SMEM, ANY] + [ANY] * len(later),
        scratch=[
            pltpu.VMEM((rows, TILE), F32),
            pltpu.VMEM((MAXT, TILE, TILE), BF16),
            pltpu.SemaphoreType.DMA,
        ],
        moved=10 << 20,
    )(users_at, items_at, live, ratings, *later)


def tile_body(counts_ref, dense_ref, items_ref, fac_ref, first_ref, second_ref, *outs):
    part_out, fac_out, first_out, second_out = outs
    fac = fac_ref[...]
    users = fac.astype(BF16)
    total = jnp.zeros((USER_ROWS, K), F32)
    upper = lax.broadcasted_iota(jnp.int32, (USER_ROWS, TILE), 0) < TILE
    for k in range(ITEM_TILES // 2):
        rows = items_ref[2 * k * TILE : 2 * (k + 1) * TILE]
        predicted = lax.dot_general(
            users, rows, (((1,), (1,)), ((), ())), preferred_element_type=F32
        )
        errors = []
        for h in range(2):
            tile = 2 * k + h
            many = jnp.where(upper, counts_ref[tile], counts_ref[ITEM_TILES + tile])
            ratings = dense_ref[tile * USER_ROWS : (tile + 1) * USER_ROWS].astype(F32)
            errors.append((predicted[:, h * TILE : (h + 1) * TILE] * many - ratings).astype(BF16))
        error = jnp.concatenate(errors, axis=1)
        total += jnp.dot(error, rows, preferred_element_type=F32)
        part = lax.dot_general(error, users, (((0,), (0,)), ((), ())), preferred_element_type=F32)
        part_out[2 * k * TILE : 2 * (k + 1) * TILE] = part.astype(BF16)
    grad = GRAD_SCALE * total + DECAY_REG * fac
    fac, first, second = adam_update(fac, first_ref[...], second_ref[...], grad)
    fac_out[...] = fac
    first_out[...] = first
    second_out[...] = second


def tile_step(counts, dense, items, state):
    return kernel_call(
        tile_body,
        [shape(ITEM_TILES * TILE, BF16)] + [shape(USER_ROWS)] * 3,
        [SMEM] + [VMEM] * (2 + len(state)),
        flops=6 * ITEM_TILES * USER_ROWS * TILE * K,
        moved=6 << 20,
    )(counts, dense, items, *state)


def per_device(
    user_factors,
    user_m,
    user_v,
    item_factors,
    item_m,
    item_v,
    ratings,
    user_tiles,
    item_tiles,
    tile_counts,
):
    item_fac, item_first, item_second = (item_factors, item_m, item_v)
    user_state = (user_factors, user_m, user_v)
    users_at, items_at = user_tiles.reshape(-1), item_tiles.reshape(-1)
    live = tile_counts.reshape(-1)
    pair = (user_tiles * ITEM_TILES + item_tiles)[0, 0]
    alive = jnp.arange(MAXT)[None, :] < live[:, None]
    named = (pair[:, :, None] == jnp.arange(PAIRS)) & alive[:, :, None]
    counts = jnp.sum(named.astype(F32), axis=1)
    for s in range(STEPS):
        current_rows = gathered(item_fac.astype(BF16))
        dense = dense_ratings(s, users_at, items_at, live, ratings)
        item_part, *user_state = tile_step(counts[s], dense, current_rows, user_state)
        item_total = summed(item_part)
        item_fac, item_first, item_second = adam_update(
            item_fac, item_first, item_second, GRAD_SCALE * item_total + DECAY_REG * item_fac
        )
        if s + 1 < STEPS:
            item_fac, item_first, item_second = shifted(
                (item_fac, item_first, item_second), "blk", -1
            )
    return (*user_state, item_fac, item_first, item_second)


def solution(mesh):
    return jax.shard_map(
        per_device,
        mesh=mesh,
        in_specs=(
            P(("blk", "narrow"), None),
            P(("blk", "narrow"), None),
            P(("blk", "narrow"), None),
            P(("blk", "narrow"), None),
            P(("blk", "narrow"), None),
            P(("blk", "narrow"), None),
            P("blk", "narrow", None, None, None, None),
            P("blk", "narrow", None, None),
            P("blk", "narrow", None, None),
            P("blk", "narrow", None),
        ),
        out_specs=(
            P(("blk", "narrow"), None),
            P(("blk", "narrow"), None),
            P(("blk", "narrow"), None),
            P(("blk", "narrow"), None),
            P(("blk", "narrow"), None),
            P(("blk", "narrow"), None),
        ),
        check_vma=False,
    )
```
